768 devices in a mesh: tp: 24 (over z, y_lo), dp: 32 (over y_hi, x, core).
Axes of the slice: x: 4, y: 8 (y_hi: 4, y_lo: 2; y = y_hi * 2 + y_lo), z: 12, core: 2. Of those that a mesh axis runs over, the one named last changes fastest.
Arguments:
- grad_out: bfloat16 [32, 480, 7168], P('dp', 'tp'), may hold values from -6 to 6
- hidden: bfloat16 [32, 480, 15360], P('dp', None, 'tp'), may hold values from -6 to 6
- weight_tiles: bfloat16 [120, 12, 128, 128], P('tp'), may hold values from -0.15625 to 0.15625
- row_list: int32 [120, 12], P('tp'), may hold values from 0 to 55, as said below
- counts: int32 [120], P('tp'), may hold values from 2 to 12, as said below
Outputs:
- grad_hidden: bfloat16 [32, 480, 15360], P('dp', None, 'tp')
- grad_tiles: float32 [120, 12, 128, 128], P('tp', None, 'dp')
The draws below stay inside these ranges and needn't reach their ends.
Inputs may be any that keep to these rules, and one draw needn't show every extreme that they name: For each block column c, the first counts[c] entries of row_list[c] are distinct; later entries are valid block rows that are not used. `counts`: some block column holds 12 tiles in every draw. The 5 block columns of each index of tp (aligned blocks of 5 columns) hold at most 45 tiles together, and the first such block holds exactly 45.
All inputs are finite; a program needn't handle non-finite values.
Results may differ from the reference program's by a relative error of at most 0.001.
Values may be sent and summed in bfloat16 or wider, within the bound.
No kernel may reach another device: no remote copies, remote signals or barrier semaphores. Data moves between devices by JAX's collectives and lax.ppermute only.
A program may use at most 128 MiB of HBM per device.

```python
import jax
import jax.numpy as jnp
from jax import lax

D = 7168
BLOCK = 128
DBLK = 56
COL_DEV = 5
NCOL = 120
FF = 15360
SLOTS = 12
LIVE_DEV = 45
GROUP = 480
N_DP = 32


def shared(key):
    count_key, order_key, total_key = jax.random.split(key, 3)
    block_count = NCOL // COL_DEV
    totals = jax.random.randint(total_key, (block_count,), 2 * COL_DEV, LIVE_DEV + 1).astype(jnp.int32)
    totals = totals.at[0].set(LIVE_DEV)
    base = jnp.full((block_count, COL_DEV), 2, jnp.int32)
    base = base.at[0, 0].set(SLOTS)
    extra = totals - jnp.sum(base, axis=1)
    positions = lax.broadcasted_iota(jnp.int32, (block_count, COL_DEV), 1)

    def one_step(step, current):
        scores = jax.random.randint(jax.random.fold_in(count_key, step), (block_count, COL_DEV), 0, 1024).astype(jnp.int32)
        scores = scores * COL_DEV + positions
        scores = jnp.where(current < SLOTS, scores, -1)
        chosen = jnp.argmax(scores, axis=1).astype(jnp.int32)
        adding = (step < extra) & (jnp.max(scores, axis=1) >= 0)
        bump = (positions == chosen[:, None]) & adding[:, None]
        return current + bump.astype(jnp.int32)
    column_counts = lax.fori_loop(0, LIVE_DEV - 2 * COL_DEV, one_step, base)
    column_counts = column_counts.reshape(NCOL).astype(jnp.int32)
    column_keys = jax.random.split(order_key, NCOL)

    def one_order(column_key):
        return jax.random.permutation(column_key, DBLK)
    orders = jax.vmap(one_order)(column_keys)
    return (column_counts, orders[:, :SLOTS].astype(jnp.int32))


def draw_row_list(key, part):
    column_counts, row_ids = shared(key)
    return row_ids


def draw_counts(key, part):
    column_counts, row_ids = shared(key)
    return column_counts


def steps_of(key, shape, cuts, low, high):
    def one(axis_at, parts):
        draws = jax.random.uniform(jax.random.fold_in(jax.random.fold_in(key, 6), axis_at), (parts,), jnp.float32, low / len(cuts), high / len(cuts))
        return jnp.repeat(jnp.exp(draws), shape[axis_at] // parts).reshape((-1,) + (1,) * (len(shape) - axis_at - 1))

    loudness = one(*cuts[0])
    for cut in cuts[1:]:
        loudness = loudness * one(*cut)
    return loudness


def scatter_about(key, shape, deviation, most, shards=(), kind=jnp.bfloat16):
    drawn = jax.random.normal(key, shape, jnp.float32) * deviation
    if len(shards) > 0:
        drawn = steps_of(key, shape, shards, -0.22, 0.18) * drawn
    return jnp.clip(drawn, min=-most, max=most).astype(kind)


def setup_inputs(seed: int = 0) -> dict:
    keys = jax.random.split(jax.random.key(seed), 6)
    grad_out = scatter_about(keys[0], (N_DP, GROUP, D), 1.0, 6.0, ((0, 32), (1, 24)))
    hidden = scatter_about(keys[1], (N_DP, GROUP, FF), 1.0, 6.0, ((0, 32), (2, 24)))
    weight_tiles = scatter_about(keys[2], (NCOL, SLOTS, BLOCK, BLOCK), (SLOTS * BLOCK) ** -0.5, 0.15625, ((0, 24),))
    row_list = draw_row_list(jax.random.fold_in(keys[5], 71), 0)
    counts = draw_counts(jax.random.fold_in(keys[5], 71), 0)
    return dict(grad_out=grad_out, hidden=hidden, weight_tiles=weight_tiles, row_list=row_list, counts=counts)


def reference(grad_out, hidden, weight_tiles, row_list, counts):
    grads = grad_out.reshape(N_DP * GROUP, DBLK, BLOCK)
    hidden_rows = hidden.reshape(N_DP * GROUP, NCOL, BLOCK)
    live_slots = lax.broadcasted_iota(jnp.int32, (NCOL, SLOTS), 1) < counts[:, None]
    norm_factor = float(N_DP * GROUP) ** -0.5

    def column(index):
        row_ids = row_list[index].astype(jnp.int32)
        picked = jnp.take(grads, row_ids, axis=1).astype(jnp.float32)
        slot_live = live_slots[index][:, None, None]
        tile_set = weight_tiles[index]
        masked = jnp.where(slot_live, tile_set, jnp.zeros_like(tile_set)).astype(jnp.float32)
        hidden_grad = jnp.einsum("tsb,sbe->te", picked, masked, precision=lax.Precision.HIGHEST)
        source = lax.dynamic_index_in_dim(hidden_rows, index, 1, keepdims=False).astype(jnp.float32)
        weight_grad = jnp.einsum("tsb,te->sbe", picked, source, precision=lax.Precision.HIGHEST)
        weight_grad = jnp.where(slot_live, weight_grad * norm_factor, jnp.zeros_like(weight_grad))
        return hidden_grad.astype(jnp.bfloat16), weight_grad

    hidden_grad, weight_grad = lax.map(column, jnp.arange(NCOL, dtype=jnp.int32))
    grad_hidden = jnp.transpose(hidden_grad, (1, 0, 2)).reshape(N_DP, GROUP, FF)
    return grad_hidden, weight_grad
```

```python
import functools

import jax
import jax.numpy as jnp
from jax import lax
from jax.experimental import pallas as pl
from jax.experimental.pallas import tpu as pltpu
from jax.sharding import Mesh, PartitionSpec as P

NZ, NYL, NYH, NX, NC = 12, 2, 4, 4, 2
COLS, SLOTS, BLOCK, DBLK = 5, 12, 128, 56
LIVE = 45
TOK = 20
SHARDS = NZ * NYL
ROWS = TOK * DBLK
MAIN = 16 * DBLK
GROUPS = NYH * NX
NORM = float(NYH * NX * NC * SHARDS * TOK) ** -0.5


def ring(n, step):
    return [(i, (i + step) % n) for i in range(n)]


def pack_rows(x):
    main = x[:16].transpose(1, 0, 2).reshape(MAIN, BLOCK)
    tail = x[16:].transpose(1, 0, 2).reshape(ROWS - MAIN, BLOCK)
    return jnp.concatenate([main, tail], 0)


def tiles_kernel(meta, rows, counts, own, *refs):
    partner = refs[:NZ]
    hid, wts, keep, send, gh_main, gh_tail, g, acc, sems = refs[NZ:]
    z, yl, core = meta[0], meta[1], meta[2]
    copies = []
    for k in range(NZ):
        copies.append(pltpu.make_async_copy(
            own.at[pl.ds(k * ROWS, ROWS)], g.at[2 * k + yl], sems.at[k]))
    for k in range(NZ):
        hop = (k + 1) // 2 if k % 2 == 1 else -(k // 2)
        src = lax.rem(z - hop + 2 * NZ, NZ)
        copies.append(pltpu.make_async_copy(
            partner[k], g.at[2 * src + (1 - yl)], sems.at[NZ + k]))
    for copy in copies:
        copy.start()
    for copy in copies:
        copy.wait()

    group_of_row = lax.broadcasted_iota(jnp.int32, (SHARDS, 16, BLOCK), 1) // 4

    def one_tile(c, s, p, first):
        b = rows[c, s]
        head = g[:, pl.ds(pl.multiple_of(b * 16, 16), 16), :]
        rest = g[:, pl.ds(pl.multiple_of(MAIN + (b // 4) * 16, 16), 16), :]
        rest = jnp.where(group_of_row == lax.rem(b, 4), rest, jnp.zeros_like(rest))
        picked = jnp.concatenate(
            [head.reshape(SHARDS * 16, BLOCK), rest.reshape(SHARDS * 16, BLOCK)], 0)
        h = hid[:, c * BLOCK:(c + 1) * BLOCK]
        wg = lax.dot_general(picked, h, (((0,), (0,)), ((), ())),
                             preferred_element_type=jnp.float32)
        for grp in range(GROUPS):
            lo, hi = wg[8 * grp:8 * grp + 4], wg[8 * grp + 4:8 * grp + 8]
            keep[grp, p] = jnp.where(core == 0, lo, hi)
            send[grp, p] = jnp.where(core == 0, hi, lo)
        part = jnp.dot(picked, wts[c, s], preferred_element_type=jnp.float32)
        if first:
            acc[...] = part
        else:
            acc[...] += part

    p = jnp.int32(0)
    for c in range(COLS):
        one_tile(c, 0, p, True)
        n = counts[c]

        def body(s, p, c=c):
            one_tile(c, s, p + s, False)
            return p

        lax.fori_loop(1, n, body, p)
        p = p + n
        cols = slice(c * BLOCK, (c + 1) * BLOCK)
        gh_main[:, :, cols] = acc[:SHARDS * 16].reshape(SHARDS, 16, BLOCK).astype(jnp.bfloat16)
        t = acc[SHARDS * 16:].reshape(SHARDS, 16, BLOCK)
        gh_tail[:, :, cols] = (t[:, 0:4] + t[:, 4:8]) + (t[:, 8:12] + t[:, 12:16])

    def clear(q, carry):
        zero = jnp.zeros((GROUPS, 4, BLOCK), jnp.float32)
        keep[:, q] = zero
        send[:, q] = zero
        return carry

    lax.fori_loop(p, LIVE, clear, 0)


def shards(grad_out, hidden, weight_tiles, row_list, counts):
    z, yl, core = lax.axis_index("z"), lax.axis_index("yl"), lax.axis_index("c")
    meta = jnp.stack([z, yl, core]).astype(jnp.int32)

    shard = pack_rows(grad_out[0].reshape(TOK, DBLK, BLOCK))
    own = lax.all_gather(shard, "z", axis=0, tiled=True)
    other = lax.ppermute(shard, "yl", ring(NYL, 1))
    partner = [other]
    up = down = other
    for k in range(6):
        up = lax.ppermute(up, "z", ring(NZ, 1))
        partner.append(up)
        if k < 5:
            down = lax.ppermute(down, "z", ring(NZ, -1))
            partner.append(down)

    h = hidden[0].reshape(SHARDS, TOK, COLS * BLOCK)
    h_main = h[:, :16].reshape(SHARDS * 16, COLS * BLOCK)
    h_tail = jnp.tile(h[:, 16:], (1, 4, 1)).reshape(SHARDS * 16, COLS * BLOCK)
    hid = jnp.concatenate([h_main, h_tail], 0)

    any_spec = pl.BlockSpec(memory_space=pl.ANY)
    smem = pl.BlockSpec(memory_space=pltpu.SMEM)
    vmem = pl.BlockSpec(memory_space=pltpu.VMEM)
    keep, send, gh_main, gh_tail = pl.pallas_call(
        tiles_kernel,
        in_specs=[smem] * 3 + [any_spec] * (NZ + 1) + [vmem] * 2,
        out_specs=[vmem] * 4,
        out_shape=[
            jax.ShapeDtypeStruct((GROUPS, LIVE, 4, BLOCK), jnp.float32),
            jax.ShapeDtypeStruct((GROUPS, LIVE, 4, BLOCK), jnp.float32),
            jax.ShapeDtypeStruct((SHARDS, 16, COLS * BLOCK), jnp.bfloat16),
            jax.ShapeDtypeStruct((SHARDS, 4, COLS * BLOCK), jnp.float32),
        ],
        scratch_shapes=[
            pltpu.VMEM((SHARDS, ROWS, BLOCK), jnp.bfloat16),
            pltpu.VMEM((SHARDS * 32, BLOCK), jnp.float32),
            pltpu.SemaphoreType.DMA((2 * NZ,)),
        ],
        compiler_params=pltpu.CompilerParams(vmem_limit_bytes=48 * 1024 * 1024),
        name="tiles",
    )(meta, row_list, counts, own, *partner, hid, weight_tiles)

    total = keep + lax.ppermute(send, "c", ring(NC, 1))
    parts = lax.all_to_all(total, ("yh", "x"), 0, 0, tiled=True)
    packed = jnp.sum(parts, axis=0) * NORM

    slot = lax.broadcasted_iota(jnp.int32, (COLS, SLOTS), 1)
    live = slot < counts[:, None]
    first = jnp.cumsum(counts) - counts
    place = jnp.where(live, first[:, None] + slot, 0)
    tiles = jnp.take(packed, place.reshape(-1), axis=0).reshape(COLS, SLOTS, 4, BLOCK)
    grad_tiles = jnp.where(live[:, :, None, None], tiles, 0.0)

    grad_hidden = jnp.concatenate([gh_main, gh_tail.astype(jnp.bfloat16)], axis=1)
    return grad_hidden.reshape(1, SHARDS * TOK, COLS * BLOCK), grad_tiles


def solution(mesh):
    fine = Mesh(mesh.devices.reshape(NZ, NYL, NYH, NX, NC), ("z", "yl", "yh", "x", "c"))
    tp, dp = ("z", "yl"), ("yh", "x", "c")
    return jax.shard_map(
        shards,
        mesh=fine,
        in_specs=(
            P(dp, tp, None),
            P(dp, None, tp),
            P(tp, None, None, None),
            P(tp, None),
            P(tp),
        ),
        out_specs=(P(dp, None, tp), P(tp, None, dp, None)),
        check_vma=False,
    )
```

```python
import functools

import jax
import jax.numpy as jnp
from jax import lax
from jax.experimental import pallas as pl
from jax.experimental.pallas import tpu as pltpu
from jax.sharding import Mesh, PartitionSpec as P

NZ, NYL, NYH, NX, NC = 12, 2, 4, 4, 2
COLS, SLOTS, BLOCK, DBLK = 5, 12, 128, 56
LIVE = 45
PAIRS = 23
TOK = 20
SHARDS = NZ * NYL
ROWS = TOK * DBLK
MAIN = 16 * DBLK
GROUPS = NYH * NX
NORM = float(NYH * NX * NC * SHARDS * TOK) ** -0.5


def ring(n, step):
    return [(i, (i + step) % n) for i in range(n)]


def pack_rows(x):
    main = x[:16].transpose(1, 0, 2).reshape(MAIN, BLOCK)
    tail = x[16:].transpose(1, 0, 2).reshape(ROWS - MAIN, BLOCK)
    return jnp.concatenate([main, tail], 0)


def load_shards(meta, column, chain, g, sems):
    z, yl = meta[0], meta[1]
    copies = []
    for k in range(NZ):
        copies.append(pltpu.make_async_copy(
            column.at[pl.ds(k * ROWS, ROWS)], g.at[2 * k + (1 - yl)], sems.at[k]))
    for k in range(NZ):
        hop = (k + 1) // 2 if k % 2 == 1 else -(k // 2)
        src = lax.rem(z - hop + 2 * NZ, NZ)
        copies.append(pltpu.make_async_copy(
            chain[k], g.at[2 * src + yl], sems.at[NZ + k]))
    for copy in copies:
        copy.start()
    for copy in copies:
        copy.wait()


def pick(g, masks, b):
    head = g[:, pl.ds(pl.multiple_of(b * 16, 16), 16), :]
    rest = g[:, pl.ds(pl.multiple_of(MAIN + (b // 4) * 16, 16), 16), :]
    rest = rest * masks[lax.rem(b, 4)][None]
    return jnp.concatenate(
        [head.reshape(SHARDS * 16, BLOCK), rest.reshape(SHARDS * 16, BLOCK)], 0)


def pick_two(g, masks, rows, c, s):
    return jnp.concatenate([pick(g, masks, rows[c, s]), pick(g, masks, rows[c, s + 1])], 1)


def weight_kernel(meta, rows, counts, masks, column, *refs):
    chain = refs[:NZ]
    hid_t, keep, send, g, tiles, sems = refs[NZ:]
    load_shards(meta, column, chain, g, sems)
    core = meta[2]
    total = jnp.int32(0)
    for c in range(COLS):
        n = counts[c]

        def body(t, carry, c=c, first=total):
            s = 2 * t
            w = jnp.dot(hid_t[c * BLOCK:(c + 1) * BLOCK, :], pick_two(g, masks, rows, c, s),
                        preferred_element_type=jnp.float32)
            tiles[first + s] = w[:, :BLOCK].T
            tiles[first + s + 1] = w[:, BLOCK:].T
            return carry

        lax.fori_loop(0, (n + 1) // 2, body, 0)
        total = total + n

    sub = lax.broadcasted_iota(jnp.int32, (GROUPS, 8, BLOCK), 1)

    def pack(q, most):
        a = jnp.where(2 * q < total, tiles[2 * q].reshape(GROUPS, 8, BLOCK), 0.0)
        b = jnp.where(2 * q + 1 < total, tiles[2 * q + 1].reshape(GROUPS, 8, BLOCK), 0.0)
        lo = jnp.where(sub < 4, a, pltpu.roll(b, 4, 1))
        hi = jnp.where(sub < 4, pltpu.roll(a, 4, 1), b)
        keep[:, q] = jnp.where(core == 0, lo, hi)
        send[:, q] = jnp.where(core == 0, hi, lo)
        return jnp.maximum(most, jnp.max(jnp.maximum(jnp.abs(a), jnp.abs(b)), axis=0))

    most = lax.fori_loop(0, PAIRS, pack, jnp.zeros((8, BLOCK), jnp.float32))
    bound = jnp.full((4, BLOCK), jnp.max(most))
    for grp in range(GROUPS):
        keep[grp, PAIRS - 1, 4:8] = bound
        send[grp, PAIRS - 1, 4:8] = bound


def hidden_kernel(meta, rows, counts, masks, column, *refs):
    chain = refs[:NZ]
    wts, gh_main, gh_tail, g, acc, sems = refs[NZ:]
    load_shards(meta, column, chain, g, sems)
    for c in range(COLS):
        n = counts[c]

        def part(s, c=c, n=n):
            second = wts[c, s + 1]
            second = jnp.where(s + 1 < n, second, jnp.zeros_like(second))
            return jnp.dot(pick_two(g, masks, rows, c, s), jnp.concatenate([wts[c, s], second], 0),
                           preferred_element_type=jnp.float32)

        acc[...] = part(0)

        def body(t, carry, part=part):
            acc[...] += part(2 * t)
            return carry

        lax.fori_loop(1, (n + 1) // 2, body, 0)
        cols = slice(c * BLOCK, (c + 1) * BLOCK)
        gh_main[:, :, cols] = acc[:SHARDS * 16].reshape(SHARDS, 16, BLOCK).astype(jnp.bfloat16)
        t = acc[SHARDS * 16:].reshape(SHARDS, 16, BLOCK)
        gh_tail[:, :, cols] = (t[:, 0:4] + t[:, 4:8]) + (t[:, 8:12] + t[:, 12:16])


def shards(grad_out, hidden, weight_tiles, row_list, counts):
    z, yl, core = lax.axis_index("z"), lax.axis_index("yl"), lax.axis_index("c")
    meta = jnp.stack([z, yl, core]).astype(jnp.int32)
    masks = jnp.repeat(jnp.eye(4, dtype=jnp.bfloat16), 4, axis=1)[:, :, None]
    masks = jnp.broadcast_to(masks, (4, 16, BLOCK))

    shard = pack_rows(grad_out[0].reshape(TOK, DBLK, BLOCK))
    other = lax.ppermute(shard, "yl", ring(NYL, 1))
    chain = [shard]
    up = down = shard
    for k in range(6):
        up = lax.ppermute(up, "z", ring(NZ, 1))
        chain.append(up)
        if k < 5:
            down = lax.ppermute(down, "z", ring(NZ, -1))
            chain.append(down)
        if k == 0:
            other, up = lax.optimization_barrier((other, up))
            column = lax.all_gather(other, "z", axis=0, tiled=True)
        if k == 2:
            h = hidden[0].T.reshape(COLS * BLOCK, SHARDS, TOK)
            h_main = h[:, :, :16].reshape(COLS * BLOCK, SHARDS * 16)
            h_tail = jnp.tile(h[:, :, 16:], (1, 1, 4)).reshape(COLS * BLOCK, SHARDS * 16)
            hid_t = jnp.concatenate([h_main, h_tail], 1)
            hid_t, up = lax.optimization_barrier((hid_t, up))

    any_spec = pl.BlockSpec(memory_space=pl.ANY)
    smem = pl.BlockSpec(memory_space=pltpu.SMEM)
    vmem = pl.BlockSpec(memory_space=pltpu.VMEM)
    params = pltpu.CompilerParams(vmem_limit_bytes=48 * 1024 * 1024)
    shard_scratch = pltpu.VMEM((SHARDS, ROWS, BLOCK), jnp.bfloat16)
    keep, send = pl.pallas_call(
        weight_kernel,
        in_specs=[smem] * 3 + [vmem] + [any_spec] * (NZ + 1) + [vmem],
        out_specs=[vmem] * 2,
        out_shape=[jax.ShapeDtypeStruct((GROUPS, PAIRS, 8, BLOCK), jnp.float32)] * 2,
        scratch_shapes=[
            shard_scratch,
            pltpu.VMEM((LIVE + 3, BLOCK, BLOCK), jnp.float32),
            pltpu.SemaphoreType.DMA((2 * NZ,)),
        ],
        compiler_params=params,
        cost_estimate=pl.CostEstimate(flops=10**9, bytes_accessed=11 * 10**6, transcendentals=0),
        name="weight_grad",
    )(meta, row_list, counts, masks, column, *chain, hid_t)

    got = lax.ppermute(send, "c", ring(NC, 1))
    bound = keep[:, PAIRS - 1:, 4:5] + got[:, PAIRS - 1:, 4:5]
    power = jnp.clip(jnp.ceil(jnp.log2(bound)), -100.0, 30.0)
    at_pair = lax.broadcasted_iota(jnp.int32, keep.shape, 1)
    at_row = lax.broadcasted_iota(jnp.int32, keep.shape, 2)
    spare = (at_pair == PAIRS - 1) & (at_row >= 4)
    coded = jnp.where(spare, power, (keep + got) * jnp.exp2(14.0 - power)).astype(jnp.float16)
    coded, meta_after = lax.optimization_barrier((coded, meta))
    parts = lax.all_to_all(coded, ("yh", "x"), 0, 0, tiled=True).astype(jnp.float32)

    gh_main, gh_tail = pl.pallas_call(
        hidden_kernel,
        in_specs=[smem] * 3 + [vmem] + [any_spec] * (NZ + 1) + [vmem],
        out_specs=[vmem] * 2,
        out_shape=[
            jax.ShapeDtypeStruct((SHARDS, 16, COLS * BLOCK), jnp.bfloat16),
            jax.ShapeDtypeStruct((SHARDS, 4, COLS * BLOCK), jnp.float32),
        ],
        scratch_shapes=[
            shard_scratch,
            pltpu.VMEM((SHARDS * 32, BLOCK), jnp.float32),
            pltpu.SemaphoreType.DMA((2 * NZ,)),
        ],
        compiler_params=params,
        cost_estimate=pl.CostEstimate(flops=10**9, bytes_accessed=10 * 10**6, transcendentals=0),
        name="hidden_grad",
    )(meta_after, row_list, counts, masks, column, *chain, weight_tiles)

    undo = jnp.exp2(parts[:, PAIRS - 1:, 4:5] - 14.0) * NORM
    packed = jnp.sum(parts * undo, axis=0).reshape(2 * PAIRS, 4, BLOCK)

    slot = lax.broadcasted_iota(jnp.int32, (COLS, SLOTS), 1)
    live = slot < counts[:, None]
    first = jnp.cumsum(counts) - counts
    place = jnp.where(live, first[:, None] + slot, 0)
    tiles = jnp.take(packed, place.reshape(-1), axis=0).reshape(COLS, SLOTS, 4, BLOCK)
    grad_tiles = jnp.where(live[:, :, None, None], tiles, 0.0)

    grad_hidden = jnp.concatenate([gh_main, gh_tail.astype(jnp.bfloat16)], axis=1)
    return grad_hidden.reshape(1, SHARDS * TOK, COLS * BLOCK), grad_tiles


def solution(mesh):
    fine = Mesh(mesh.devices.reshape(NZ, NYL, NYH, NX, NC), ("z", "yl", "yh", "x", "c"))
    tp, dp = ("z", "yl"), ("yh", "x", "c")
    return jax.shard_map(
        shards,
        mesh=fine,
        in_specs=(
            P(dp, tp, None),
            P(dp, None, tp),
            P(tp, None, None, None),
            P(tp, None),
            P(tp),
        ),
        out_specs=(P(dp, None, tp), P(tp, None, dp, None)),
        check_vma=False,
    )
```

```python
import functools

import jax
import jax.numpy as jnp
from jax import lax
from jax.experimental import pallas as pl
from jax.experimental.pallas import tpu as pltpu
from jax.sharding import Mesh, PartitionSpec as P

NZ, NYL, NYH, NX, NC = 12, 2, 4, 4, 2
COLS, SLOTS, BLOCK, DBLK = 5, 12, 128, 56
LIVE = 45
PAIRS = 23
TOK = 20
SHARDS = NZ * NYL
ROWS = TOK * DBLK
MAIN = 16 * DBLK
GROUPS = NYH * NX
NORM = float(NYH * NX * NC * SHARDS * TOK) ** -0.5


def ring(n, step):
    return [(i, (i + step) % n) for i in range(n)]


def pack_rows(x):
    main = x[:16].transpose(1, 0, 2).reshape(MAIN, BLOCK)
    tail = x[16:].transpose(1, 0, 2).reshape(ROWS - MAIN, BLOCK)
    return jnp.concatenate([main, tail], 0)


def load_shards(meta, moved, g, sems):
    z, yl = meta[0], meta[1]
    copies = []
    for i, ref in enumerate(moved):
        k = i % NZ
        hop = (k + 1) // 2 if k % 2 == 1 else -(k // 2)
        src = lax.rem(z - hop + NZ, NZ)
        column = yl if i < NZ else 1 - yl
        copies.append(pltpu.make_async_copy(ref, g.at[2 * src + column], sems.at[i]))
    for copy in copies:
        copy.start()
    for copy in copies:
        copy.wait()


def pick(g, masks, b):
    head = g[:, pl.ds(pl.multiple_of(b * 16, 16), 16), :]
    rest = g[:, pl.ds(pl.multiple_of(MAIN + (b // 4) * 16, 16), 16), :]
    rest = rest * masks[lax.rem(b, 4)][None]
    return jnp.concatenate(
        [head.reshape(SHARDS * 16, BLOCK), rest.reshape(SHARDS * 16, BLOCK)], 0)


def pick_two(g, masks, rows, c, s):
    return jnp.concatenate([pick(g, masks, rows[c, s]), pick(g, masks, rows[c, s + 1])], 1)


def weight_kernel(meta, rows, counts, masks, *refs):
    moved, refs = refs[:SHARDS], refs[SHARDS:]
    hid_t, keep, send, g, tiles, sems = refs
    load_shards(meta, moved, g, sems)
    core = meta[2]
    total = jnp.int32(0)
    for c in range(COLS):
        n = counts[c]

        def body(t, carry, c=c, first=total):
            s = 2 * t
            w = jnp.dot(hid_t[c * BLOCK:(c + 1) * BLOCK, :], pick_two(g, masks, rows, c, s),
                        preferred_element_type=jnp.float32)
            tiles[first + s] = w[:, :BLOCK].T
            tiles[first + s + 1] = w[:, BLOCK:].T
            return carry

        lax.fori_loop(0, (n + 1) // 2, body, 0)
        total = total + n

    sub = lax.broadcasted_iota(jnp.int32, (GROUPS, 8, BLOCK), 1)

    def pack(q, most):
        a = jnp.where(2 * q < total, tiles[2 * q].reshape(GROUPS, 8, BLOCK), 0.0)
        b = jnp.where(2 * q + 1 < total, tiles[2 * q + 1].reshape(GROUPS, 8, BLOCK), 0.0)
        lo = jnp.where(sub < 4, a, pltpu.roll(b, 4, 1))
        hi = jnp.where(sub < 4, pltpu.roll(a, 4, 1), b)
        keep[:, q] = jnp.where(core == 0, lo, hi)
        send[:, q] = jnp.where(core == 0, hi, lo)
        return jnp.maximum(most, jnp.max(jnp.maximum(jnp.abs(a), jnp.abs(b)), axis=0))

    most = lax.fori_loop(0, PAIRS, pack, jnp.zeros((8, BLOCK), jnp.float32))
    bound = jnp.full((4, BLOCK), jnp.max(most))
    for grp in range(GROUPS):
        keep[grp, PAIRS - 1, 4:8] = bound
        send[grp, PAIRS - 1, 4:8] = bound


def hidden_kernel(meta, rows, counts, masks, *refs):
    moved, refs = refs[:SHARDS], refs[SHARDS:]
    wts, gh_main, gh_tail, g, acc, sems = refs
    load_shards(meta, moved, g, sems)
    for c in range(COLS):
        n = counts[c]

        def part(s, c=c, n=n):
            second = wts[c, s + 1]
            second = jnp.where(s + 1 < n, second, jnp.zeros_like(second))
            return jnp.dot(pick_two(g, masks, rows, c, s), jnp.concatenate([wts[c, s], second], 0),
                           preferred_element_type=jnp.float32)

        acc[...] = part(0)

        def body(t, carry, part=part):
            acc[...] += part(2 * t)
            return carry

        lax.fori_loop(1, (n + 1) // 2, body, 0)
        cols = slice(c * BLOCK, (c + 1) * BLOCK)
        gh_main[:, :, cols] = acc[:SHARDS * 16].reshape(SHARDS, 16, BLOCK).astype(jnp.bfloat16)
        t = acc[SHARDS * 16:].reshape(SHARDS, 16, BLOCK)
        gh_tail[:, :, cols] = (t[:, 0:4] + t[:, 4:8]) + (t[:, 8:12] + t[:, 12:16])


def shards(grad_out, hidden, weight_tiles, row_list, counts):
    z, yl, core = lax.axis_index("z"), lax.axis_index("yl"), lax.axis_index("c")
    meta = jnp.stack([z, yl, core]).astype(jnp.int32)
    masks = jnp.repeat(jnp.eye(4, dtype=jnp.bfloat16), 4, axis=1)[:, :, None]
    masks = jnp.broadcast_to(masks, (4, 16, BLOCK))

    shard = pack_rows(grad_out[0].reshape(TOK, DBLK, BLOCK))
    other = lax.ppermute(shard, "yl", ring(NYL, 1))
    moved = []
    for start in (shard, other):
        up = down = start
        moved.append(start)
        for k in range(6):
            up = lax.ppermute(up, "z", ring(NZ, 1))
            moved.append(up)
            if k < 5:
                down = lax.ppermute(down, "z", ring(NZ, -1))
                moved.append(down)

    t = lax.broadcasted_iota(jnp.int32, (SHARDS * TOK, SHARDS * 32), 0)
    k = lax.broadcasted_iota(jnp.int32, (SHARDS * TOK, SHARDS * 32), 1)
    j = k % (SHARDS * 16)
    place = j // 16 * TOK + jnp.where(k < SHARDS * 16, j % 16, 16 + j % 4)
    hid_t = lax.dot_general(hidden[0], (t == place).astype(jnp.bfloat16), (((0,), (0,)), ((), ())))

    any_spec = pl.BlockSpec(memory_space=pl.ANY)
    smem = pl.BlockSpec(memory_space=pltpu.SMEM)
    vmem = pl.BlockSpec(memory_space=pltpu.VMEM)
    params = pltpu.CompilerParams(vmem_limit_bytes=62 * 1024 * 1024)
    shard_scratch = pltpu.VMEM((SHARDS, ROWS, BLOCK), jnp.bfloat16)
    keep, send = pl.pallas_call(
        weight_kernel,
        in_specs=[smem] * 3 + [vmem] + [any_spec] * SHARDS + [vmem],
        out_specs=[vmem] * 2,
        out_shape=[jax.ShapeDtypeStruct((GROUPS, PAIRS, 8, BLOCK), jnp.float32)] * 2,
        scratch_shapes=[
            shard_scratch,
            pltpu.VMEM((LIVE + 3, BLOCK, BLOCK), jnp.float32),
            pltpu.SemaphoreType.DMA((SHARDS,)),
        ],
        compiler_params=params,
        cost_estimate=pl.CostEstimate(flops=10**9, bytes_accessed=11 * 10**6, transcendentals=0),
        name="weight_grad",
    )(meta, row_list, counts, masks, *moved, hid_t)

    got = lax.ppermute(send, "c", ring(NC, 1))
    bound = keep[:, PAIRS - 1:, 4:5] + got[:, PAIRS - 1:, 4:5]
    power = jnp.clip(jnp.ceil(jnp.log2(bound)), -100.0, 30.0)
    at_pair = lax.broadcasted_iota(jnp.int32, keep.shape, 1)
    at_row = lax.broadcasted_iota(jnp.int32, keep.shape, 2)
    spare = (at_pair == PAIRS - 1) & (at_row >= 4)
    coded = jnp.where(spare, power, (keep + got) * jnp.exp2(14.0 - power)).astype(jnp.float16)
    coded, meta_after = lax.optimization_barrier((coded, meta))
    parts = lax.all_to_all(coded, ("yh", "x"), 0, 0, tiled=True)

    gh_main, gh_tail = pl.pallas_call(
        hidden_kernel,
        in_specs=[smem] * 3 + [vmem] + [any_spec] * SHARDS + [vmem],
        out_specs=[vmem] * 2,
        out_shape=[
            jax.ShapeDtypeStruct((SHARDS, 16, COLS * BLOCK), jnp.bfloat16),
            jax.ShapeDtypeStruct((SHARDS, 4, COLS * BLOCK), jnp.float32),
        ],
        scratch_shapes=[
            shard_scratch,
            pltpu.VMEM((SHARDS * 32, BLOCK), jnp.float32),
            pltpu.SemaphoreType.DMA((SHARDS,)),
        ],
        compiler_params=params,
        cost_estimate=pl.CostEstimate(flops=10**9, bytes_accessed=10 * 10**6, transcendentals=0),
        name="hidden_grad",
    )(meta_after, row_list, counts, masks, *moved, weight_tiles)

    undo = jnp.exp2(parts[:, PAIRS - 1:, 4:5].astype(jnp.float32) - 14.0) * NORM
    packed = jnp.sum(parts.astype(jnp.float32) * undo, axis=0).reshape(2 * PAIRS, 4, BLOCK)

    slot = lax.broadcasted_iota(jnp.int32, (COLS, SLOTS), 1)
    live = slot < counts[:, None]
    first = jnp.cumsum(counts) - counts
    place = jnp.where(live, first[:, None] + slot, 0)
    tiles = jnp.take(packed, place.reshape(-1), axis=0).reshape(COLS, SLOTS, 4, BLOCK)
    grad_tiles = jnp.where(live[:, :, None, None], tiles, 0.0)

    grad_hidden = jnp.concatenate([gh_main, gh_tail.astype(jnp.bfloat16)], axis=1)
    return grad_hidden.reshape(1, SHARDS * TOK, COLS * BLOCK), grad_tiles


def solution(mesh):
    fine = Mesh(mesh.devices.reshape(NZ, NYL, NYH, NX, NC), ("z", "yl", "yh", "x", "c"))
    tp, dp = ("z", "yl"), ("yh", "x", "c")
    return jax.shard_map(
        shards,
        mesh=fine,
        in_specs=(
            P(dp, tp, None),
            P(dp, None, tp),
            P(tp, None, None, None),
            P(tp, None),
            P(tp),
        ),
        out_specs=(P(dp, None, tp), P(tp, None, dp, None)),
        check_vma=False,
    )
```

```python
import functools

import jax
import jax.numpy as jnp
from jax import lax
from jax.experimental import pallas as pl
from jax.experimental.pallas import tpu as pltpu
from jax.sharding import Mesh, PartitionSpec as P

NZ, NYL, NYH, NX, NC = 12, 2, 4, 4, 2
COLS, SLOTS, BLOCK, DBLK = 5, 12, 128, 56
LIVE = 45
PAIRS = 23
TOK = 20
SHARDS = NZ * NYL
ROWS = TOK * DBLK
MAIN = 16 * DBLK
GROUPS = NYH * NX
NORM = float(NYH * NX * NC * SHARDS * TOK) ** -0.5


def ring(n, step):
    return [(i, (i + step) % n) for i in range(n)]


def pack_rows(x):
    main = x[:16].transpose(1, 0, 2).reshape(MAIN, BLOCK)
    tail = x[16:].transpose(1, 0, 2).reshape(ROWS - MAIN, BLOCK)
    return jnp.concatenate([main, tail], 0)


def load_shards(meta, moved, g, sems):
    z, yl = meta[0], meta[1]
    copies = []
    for i, ref in enumerate(moved):
        k = i % NZ
        hop = (k + 1) // 2 if k % 2 == 1 else -(k // 2)
        src = lax.rem(z - hop + NZ, NZ)
        column = yl if i < NZ else 1 - yl
        copies.append(pltpu.make_async_copy(ref, g.at[2 * src + column], sems.at[i]))
    for copy in copies:
        copy.start()
    for copy in copies:
        copy.wait()


def pick(g, masks, b):
    head = g[:, pl.ds(pl.multiple_of(b * 16, 16), 16), :]
    rest = g[:, pl.ds(pl.multiple_of(MAIN + (b // 4) * 16, 16), 16), :]
    rest = rest * masks[lax.rem(b, 4)][None]
    return jnp.concatenate(
        [head.reshape(SHARDS * 16, BLOCK), rest.reshape(SHARDS * 16, BLOCK)], 0)


def pick_two(g, masks, rows, c, s):
    return jnp.concatenate([pick(g, masks, rows[c, s]), pick(g, masks, rows[c, s + 1])], 1)


def weight_kernel(meta, rows, counts, masks, *refs):
    moved, refs = refs[:SHARDS], refs[SHARDS:]
    hid_t, keep, send, g, tiles, sems = refs
    load_shards(meta, moved, g, sems)
    core = meta[2]
    total = jnp.int32(0)
    for c in range(COLS):
        n = counts[c]

        def body(t, carry, c=c, first=total):
            s = 4 * t
            h = hid_t[c * BLOCK:(c + 1) * BLOCK, :]
            ws = [jnp.dot(h, pick_two(g, masks, rows, c, s + i), preferred_element_type=jnp.float32)
                  for i in (0, 2)]
            for i, w in enumerate(ws):
                tiles[first + s + 2 * i] = w[:, :BLOCK].T
                tiles[first + s + 2 * i + 1] = w[:, BLOCK:].T
            return carry

        lax.fori_loop(0, (n + 3) // 4, body, 0)
        total = total + n

    sub = lax.broadcasted_iota(jnp.int32, (GROUPS, 8, BLOCK), 1)

    def pack(q, most):
        a = jnp.where(2 * q < total, tiles[2 * q].reshape(GROUPS, 8, BLOCK), 0.0)
        b = jnp.where(2 * q + 1 < total, tiles[2 * q + 1].reshape(GROUPS, 8, BLOCK), 0.0)
        lo = jnp.where(sub < 4, a, pltpu.roll(b, 4, 1))
        hi = jnp.where(sub < 4, pltpu.roll(a, 4, 1), b)
        keep[:, q] = jnp.where(core == 0, lo, hi)
        send[:, q] = jnp.where(core == 0, hi, lo)
        return jnp.maximum(most, jnp.max(jnp.maximum(jnp.abs(a), jnp.abs(b)), axis=0))

    most = lax.fori_loop(0, PAIRS, pack, jnp.zeros((8, BLOCK), jnp.float32))
    bound = jnp.full((4, BLOCK), jnp.max(most))
    for grp in range(GROUPS):
        keep[grp, PAIRS - 1, 4:8] = bound
        send[grp, PAIRS - 1, 4:8] = bound


def hidden_kernel(meta, rows, counts, masks, *refs):
    moved, refs = refs[:SHARDS], refs[SHARDS:]
    wts, gh_main, gh_tail, g, acc, sems = refs
    load_shards(meta, moved, g, sems)
    for c in range(COLS):
        n = counts[c]

        def part(s, c=c, n=n):
            parts = [wts[c, s]]
            for i in (1, 2, 3):
                w = wts[c, s + i]
                parts.append(jnp.where(s + i < n, w, jnp.zeros_like(w)))
            picked = jnp.concatenate(
                [pick_two(g, masks, rows, c, s), pick_two(g, masks, rows, c, s + 2)], 1)
            return jnp.dot(picked, jnp.concatenate(parts, 0), preferred_element_type=jnp.float32)

        acc[...] = part(0)

        def body(t, carry, part=part):
            acc[...] += part(4 * t)
            return carry

        lax.fori_loop(1, (n + 3) // 4, body, 0)
        cols = slice(c * BLOCK, (c + 1) * BLOCK)
        gh_main[:, :, cols] = acc[:SHARDS * 16].reshape(SHARDS, 16, BLOCK).astype(jnp.bfloat16)
        t = acc[SHARDS * 16:].reshape(SHARDS, 16, BLOCK)
        gh_tail[:, :, cols] = (t[:, 0:4] + t[:, 4:8]) + (t[:, 8:12] + t[:, 12:16])


def shards(grad_out, hidden, weight_tiles, row_list, counts):
    z, yl, core = lax.axis_index("z"), lax.axis_index("yl"), lax.axis_index("c")
    meta = jnp.stack([z, yl, core]).astype(jnp.int32)
    masks = jnp.repeat(jnp.eye(4, dtype=jnp.bfloat16), 4, axis=1)[:, :, None]
    masks = jnp.broadcast_to(masks, (4, 16, BLOCK))

    shard = pack_rows(grad_out[0].reshape(TOK, DBLK, BLOCK))
    other = lax.ppermute(shard, "yl", ring(NYL, 1))
    moved = []
    for mine in (True, False):
        start = shard if mine else other
        up = down = start
        moved.append(start)
        for k in range(6):
            if k < 5 or mine:
                up = lax.ppermute(up, "z", ring(NZ, 1))
                moved.append(up)
            if k < 5 or not mine:
                down = lax.ppermute(down, "z", ring(NZ, -1))
                moved.append(down)
            if k == 0 and mine:
                other, down = lax.optimization_barrier((other, down))

    t = lax.broadcasted_iota(jnp.int32, (SHARDS * TOK, SHARDS * 32), 0)
    k = lax.broadcasted_iota(jnp.int32, (SHARDS * TOK, SHARDS * 32), 1)
    j = k % (SHARDS * 16)
    place = j // 16 * TOK + jnp.where(k < SHARDS * 16, j % 16, 16 + j % 4)
    hid_t = lax.dot_general(hidden[0], (t == place).astype(jnp.bfloat16), (((0,), (0,)), ((), ())))

    any_spec = pl.BlockSpec(memory_space=pl.ANY)
    smem = pl.BlockSpec(memory_space=pltpu.SMEM)
    vmem = pl.BlockSpec(memory_space=pltpu.VMEM)
    params = pltpu.CompilerParams(vmem_limit_bytes=62 * 1024 * 1024)
    shard_scratch = pltpu.VMEM((SHARDS, ROWS, BLOCK), jnp.bfloat16)
    keep, send = pl.pallas_call(
        weight_kernel,
        in_specs=[smem] * 3 + [vmem] + [any_spec] * SHARDS + [vmem],
        out_specs=[vmem] * 2,
        out_shape=[jax.ShapeDtypeStruct((GROUPS, PAIRS, 8, BLOCK), jnp.float32)] * 2,
        scratch_shapes=[
            shard_scratch,
            pltpu.VMEM((LIVE + 3, BLOCK, BLOCK), jnp.float32),
            pltpu.SemaphoreType.DMA((SHARDS,)),
        ],
        compiler_params=params,
        cost_estimate=pl.CostEstimate(flops=10**9, bytes_accessed=11 * 10**6, transcendentals=0),
        name="weight_grad",
    )(meta, row_list, counts, masks, *moved, hid_t)

    got = lax.ppermute(send, "c", ring(NC, 1))
    bound = keep[:, PAIRS - 1:, 4:5] + got[:, PAIRS - 1:, 4:5]
    power = jnp.clip(jnp.ceil(jnp.log2(bound)), -100.0, 30.0)
    at_pair = lax.broadcasted_iota(jnp.int32, keep.shape, 1)
    at_row = lax.broadcasted_iota(jnp.int32, keep.shape, 2)
    spare = (at_pair == PAIRS - 1) & (at_row >= 4)
    coded = jnp.where(spare, power, (keep + got) * jnp.exp2(14.0 - power)).astype(jnp.float16)
    coded, meta_after = lax.optimization_barrier((coded, meta))
    parts = lax.all_to_all(coded, ("yh", "x"), 0, 0, tiled=True)

    gh_main, gh_tail = pl.pallas_call(
        hidden_kernel,
        in_specs=[smem] * 3 + [vmem] + [any_spec] * SHARDS + [vmem],
        out_specs=[vmem] * 2,
        out_shape=[
            jax.ShapeDtypeStruct((SHARDS, 16, COLS * BLOCK), jnp.bfloat16),
            jax.ShapeDtypeStruct((SHARDS, 4, COLS * BLOCK), jnp.float32),
        ],
        scratch_shapes=[
            shard_scratch,
            pltpu.VMEM((SHARDS * 32, BLOCK), jnp.float32),
            pltpu.SemaphoreType.DMA((SHARDS,)),
        ],
        compiler_params=params,
        cost_estimate=pl.CostEstimate(flops=10**9, bytes_accessed=10 * 10**6, transcendentals=0),
        name="hidden_grad",
    )(meta_after, row_list, counts, masks, *moved, weight_tiles)

    undo = jnp.exp2(parts[:, PAIRS - 1:, 4:5].astype(jnp.float32) - 14.0) * NORM
    packed = jnp.sum(parts.astype(jnp.float32) * undo, axis=0).reshape(2 * PAIRS, 4, BLOCK)

    slot = lax.broadcasted_iota(jnp.int32, (COLS, SLOTS), 1)
    live = slot < counts[:, None]
    first = jnp.cumsum(counts) - counts
    place = jnp.where(live, first[:, None] + slot, 0)
    tiles = jnp.take(packed, place.reshape(-1), axis=0).reshape(COLS, SLOTS, 4, BLOCK)
    grad_tiles = jnp.where(live[:, :, None, None], tiles, 0.0)

    grad_hidden = jnp.concatenate([gh_main, gh_tail.astype(jnp.bfloat16)], axis=1)
    return grad_hidden.reshape(1, SHARDS * TOK, COLS * BLOCK), grad_tiles


def solution(mesh):
    fine = Mesh(mesh.devices.reshape(NZ, NYL, NYH, NX, NC), ("z", "yl", "yh", "x", "c"))
    tp, dp = ("z", "yl"), ("yh", "x", "c")
    return jax.shard_map(
        shards,
        mesh=fine,
        in_specs=(
            P(dp, tp, None),
            P(dp, None, tp),
            P(tp, None, None, None),
            P(tp, None),
            P(tp),
        ),
        out_specs=(P(dp, None, tp), P(tp, None, dp, None)),
        check_vma=False,
    )
```

```python
import functools

import jax
import jax.numpy as jnp
import ml_dtypes
import numpy as np
from jax import lax
from jax.experimental import pallas as pl
from jax.experimental.pallas import tpu as pltpu
from jax.sharding import Mesh, PartitionSpec as P

NZ, NYL, NYH, NX, NC = 12, 2, 4, 4, 2
COLS, SLOTS, BLOCK, DBLK = 5, 12, 128, 56
LIVE = 45
PAIRS = 23
TOK = 20
SHARDS = NZ * NYL
ROWS = TOK * DBLK
MAIN = 16 * DBLK
GROUPS = NYH * NX
NORM = float(NYH * NX * NC * SHARDS * TOK) ** -0.5


def ring(n, step):
    return [(i, (i + step) % n) for i in range(n)]


def pack_rows(x):
    main = x[:16].transpose(1, 0, 2).reshape(MAIN, BLOCK)
    tail = x[16:].transpose(1, 0, 2).reshape(ROWS - MAIN, BLOCK)
    return jnp.concatenate([main, tail], 0)


def load_shards(meta, moved, g, sems):
    z, yl = meta[0], meta[1]
    copies = []
    for i, ref in enumerate(moved):
        k = i % NZ
        hop = (k + 1) // 2 if k % 2 == 1 else -(k // 2)
        src = lax.rem(z - hop + NZ, NZ)
        column = yl if i < NZ else 1 - yl
        copies.append(pltpu.make_async_copy(ref, g.at[2 * src + column], sems.at[i]))
    for copy in copies:
        copy.start()
    for copy in copies:
        copy.wait()


def pick(g, masks, b):
    head = g[:, pl.ds(pl.multiple_of(b * 16, 16), 16), :]
    rest = g[:, pl.ds(pl.multiple_of(MAIN + (b // 4) * 16, 16), 16), :]
    rest = rest * masks[lax.rem(b, 4)][None]
    return jnp.concatenate(
        [head.reshape(SHARDS * 16, BLOCK), rest.reshape(SHARDS * 16, BLOCK)], 0)


def pick_two(g, masks, rows, c, s):
    return jnp.concatenate([pick(g, masks, rows[c, s]), pick(g, masks, rows[c, s + 1])], 1)


def weight_kernel(meta, rows, counts, masks, *refs):
    moved, refs = refs[:SHARDS], refs[SHARDS:]
    hid_t, keep, send, g, tiles, sems = refs
    load_shards(meta, moved, g, sems)
    core = meta[2]
    total = jnp.int32(0)
    for c in range(COLS):
        n = counts[c]

        def body(t, carry, c=c, first=total):
            s = 6 * t
            h = hid_t[c * BLOCK:(c + 1) * BLOCK, :]
            ws = [jnp.dot(h, pick_two(g, masks, rows, c, s + i), preferred_element_type=jnp.float32)
                  for i in (0, 2, 4)]
            for i, w in enumerate(ws):
                tiles[first + s + 2 * i] = w[:, :BLOCK].T
                tiles[first + s + 2 * i + 1] = w[:, BLOCK:].T
            return carry

        lax.fori_loop(0, (n + 5) // 6, body, 0)
        total = total + n

    sub = lax.broadcasted_iota(jnp.int32, (GROUPS, 8, BLOCK), 1)

    def pack(q, most):
        a = jnp.where(2 * q < total, tiles[2 * q].reshape(GROUPS, 8, BLOCK), 0.0)
        b = jnp.where(2 * q + 1 < total, tiles[2 * q + 1].reshape(GROUPS, 8, BLOCK), 0.0)
        lo = jnp.where(sub < 4, a, pltpu.roll(b, 4, 1))
        hi = jnp.where(sub < 4, pltpu.roll(a, 4, 1), b)
        keep[:, q] = jnp.where(core == 0, lo, hi)
        send[:, q] = jnp.where(core == 0, hi, lo)
        return jnp.maximum(most, jnp.max(jnp.maximum(jnp.abs(a), jnp.abs(b)), axis=0))

    most = lax.fori_loop(0, PAIRS, pack, jnp.zeros((8, BLOCK), jnp.float32))
    bound = jnp.full((4, BLOCK), jnp.max(most))
    for grp in range(GROUPS):
        keep[grp, PAIRS - 1, 4:8] = bound
        send[grp, PAIRS - 1, 4:8] = bound


def hidden_kernel(meta, rows, counts, masks, *refs):
    moved, refs = refs[:SHARDS], refs[SHARDS:]
    wts, gh_main, gh_tail, g, acc, sems = refs
    load_shards(meta, moved, g, sems)
    for c in range(COLS):
        n = counts[c]

        def part(s, c=c, n=n):
            parts = [wts[c, s]]
            for i in (1, 2, 3):
                w = wts[c, s + i]
                parts.append(jnp.where(s + i < n, w, jnp.zeros_like(w)))
            picked = jnp.concatenate(
                [pick_two(g, masks, rows, c, s), pick_two(g, masks, rows, c, s + 2)], 1)
            return jnp.dot(picked, jnp.concatenate(parts, 0), preferred_element_type=jnp.float32)

        acc[...] = part(0)

        def body(t, carry, part=part):
            acc[...] += part(4 * t)
            return carry

        lax.fori_loop(1, (n + 3) // 4, body, 0)
        cols = slice(c * BLOCK, (c + 1) * BLOCK)
        gh_main[:, :, cols] = acc[:SHARDS * 16].reshape(SHARDS, 16, BLOCK).astype(jnp.bfloat16)
        t = acc[SHARDS * 16:].reshape(SHARDS, 16, BLOCK)
        gh_tail[:, :, cols] = (t[:, 0:4] + t[:, 4:8]) + (t[:, 8:12] + t[:, 12:16])


def shards(grad_out, hidden, weight_tiles, row_list, counts):
    z, yl, core = lax.axis_index("z"), lax.axis_index("yl"), lax.axis_index("c")
    meta = jnp.stack([z, yl, core]).astype(jnp.int32)
    masks = np.repeat(np.eye(4), 4, axis=1)[:, :, None].repeat(BLOCK, axis=2)
    masks = jnp.asarray(masks.astype(ml_dtypes.bfloat16))

    shard = pack_rows(grad_out[0].reshape(TOK, DBLK, BLOCK))
    other = lax.ppermute(shard, "yl", ring(NYL, 1))
    moved = []
    for mine in (True, False):
        start = shard if mine else other
        up = down = start
        moved.append(start)
        for k in range(6):
            if k < 5 or mine:
                up = lax.ppermute(up, "z", ring(NZ, 1))
                moved.append(up)
            if k < 5 or not mine:
                down = lax.ppermute(down, "z", ring(NZ, -1))
                moved.append(down)
            if k == 0 and mine:
                other, down = lax.optimization_barrier((other, down))

    t = lax.broadcasted_iota(jnp.int32, (SHARDS * TOK, SHARDS * 32), 0)
    k = lax.broadcasted_iota(jnp.int32, (SHARDS * TOK, SHARDS * 32), 1)
    j = k % (SHARDS * 16)
    place = j // 16 * TOK + jnp.where(k < SHARDS * 16, j % 16, 16 + j % 4)
    hid_t = lax.dot_general(hidden[0], (t == place).astype(jnp.bfloat16), (((0,), (0,)), ((), ())))

    any_spec = pl.BlockSpec(memory_space=pl.ANY)
    smem = pl.BlockSpec(memory_space=pltpu.SMEM)
    vmem = pl.BlockSpec(memory_space=pltpu.VMEM)
    params = pltpu.CompilerParams(vmem_limit_bytes=62 * 1024 * 1024)
    shard_scratch = pltpu.VMEM((SHARDS, ROWS, BLOCK), jnp.bfloat16)
    keep, send = pl.pallas_call(
        weight_kernel,
        in_specs=[smem] * 3 + [vmem] + [any_spec] * SHARDS + [vmem],
        out_specs=[vmem] * 2,
        out_shape=[jax.ShapeDtypeStruct((GROUPS, PAIRS, 8, BLOCK), jnp.float32)] * 2,
        scratch_shapes=[
            shard_scratch,
            pltpu.VMEM((LIVE + 5, BLOCK, BLOCK), jnp.float32),
            pltpu.SemaphoreType.DMA((SHARDS,)),
        ],
        compiler_params=params,
        cost_estimate=pl.CostEstimate(flops=10**9, bytes_accessed=11 * 10**6, transcendentals=0),
        name="weight_grad",
    )(meta, row_list, counts, masks, *moved, hid_t)

    got = lax.ppermute(send, "c", ring(NC, 1))
    bound = keep[:, PAIRS - 1:, 4:5] + got[:, PAIRS - 1:, 4:5]
    power = jnp.clip(jnp.ceil(jnp.log2(bound)), -100.0, 30.0)
    at_pair = lax.broadcasted_iota(jnp.int32, keep.shape, 1)
    at_row = lax.broadcasted_iota(jnp.int32, keep.shape, 2)
    spare = (at_pair == PAIRS - 1) & (at_row >= 4)
    coded = jnp.where(spare, power, (keep + got) * jnp.exp2(14.0 - power)).astype(jnp.float16)
    coded, meta_after = lax.optimization_barrier((coded, meta))
    parts = lax.all_to_all(coded, ("yh", "x"), 0, 0, tiled=True)

    gh_main, gh_tail = pl.pallas_call(
        hidden_kernel,
        in_specs=[smem] * 3 + [vmem] + [any_spec] * SHARDS + [vmem],
        out_specs=[vmem] * 2,
        out_shape=[
            jax.ShapeDtypeStruct((SHARDS, 16, COLS * BLOCK), jnp.bfloat16),
            jax.ShapeDtypeStruct((SHARDS, 4, COLS * BLOCK), jnp.float32),
        ],
        scratch_shapes=[
            shard_scratch,
            pltpu.VMEM((SHARDS * 32, BLOCK), jnp.float32),
            pltpu.SemaphoreType.DMA((SHARDS,)),
        ],
        compiler_params=params,
        cost_estimate=pl.CostEstimate(flops=10**9, bytes_accessed=10 * 10**6, transcendentals=0),
        name="hidden_grad",
    )(meta_after, row_list, counts, masks, *moved, weight_tiles)

    undo = jnp.exp2(parts[:, PAIRS - 1:, 4:5].astype(jnp.float32) - 14.0) * NORM
    packed = jnp.sum(parts.astype(jnp.float32) * undo, axis=0).reshape(2 * PAIRS, 4, BLOCK)

    slot = lax.broadcasted_iota(jnp.int32, (COLS, SLOTS), 1)
    live = slot < counts[:, None]
    first = jnp.cumsum(counts) - counts
    place = jnp.where(live, first[:, None] + slot, 0)
    tiles = jnp.take(packed, place.reshape(-1), axis=0, mode="clip").reshape(COLS, SLOTS, 4, BLOCK)
    grad_tiles = jnp.where(live[:, :, None, None], tiles, 0.0)

    grad_hidden = jnp.concatenate([gh_main, gh_tail.astype(jnp.bfloat16)], axis=1)
    return grad_hidden.reshape(1, SHARDS * TOK, COLS * BLOCK), grad_tiles


def solution(mesh):
    fine = Mesh(mesh.devices.reshape(NZ, NYL, NYH, NX, NC), ("z", "yl", "yh", "x", "c"))
    tp, dp = ("z", "yl"), ("yh", "x", "c")
    return jax.shard_map(
        shards,
        mesh=fine,
        in_specs=(
            P(dp, tp, None),
            P(dp, None, tp),
            P(tp, None, None, None),
            P(tp, None),
            P(tp),
        ),
        out_specs=(P(dp, None, tp), P(tp, None, dp, None)),
        check_vma=False,
    )
```

```python
import functools

import jax
import jax.numpy as jnp
import ml_dtypes
import numpy as np
from jax import lax
from jax.experimental import pallas as pl
from jax.experimental.pallas import tpu as pltpu
from jax.sharding import Mesh, PartitionSpec as P

NZ, NYL, NYH, NX, NC = 12, 2, 4, 4, 2
COLS, SLOTS, BLOCK, DBLK = 5, 12, 128, 56
LIVE = 45
PAIRS = 23
TOK = 20
SHARDS = NZ * NYL
ROWS = TOK * DBLK
MAIN = 16 * DBLK
GROUPS = NYH * NX
NORM = float(NYH * NX * NC * SHARDS * TOK) ** -0.5


def ring(n, step):
    return [(i, (i + step) % n) for i in range(n)]


def pack_rows(x):
    main = x[:16].transpose(1, 0, 2).reshape(MAIN, BLOCK)
    tail = x[16:].transpose(1, 0, 2).reshape(ROWS - MAIN, BLOCK)
    return jnp.concatenate([main, tail], 0)


def load_shards(meta, moved, g, sems):
    z, yl = meta[0], meta[1]
    copies = []
    for i, ref in enumerate(moved):
        k = i % NZ
        hop = (k + 1) // 2 if k % 2 == 1 else -(k // 2)
        src = lax.rem(z - hop + NZ, NZ)
        column = yl if i < NZ else 1 - yl
        copies.append(pltpu.make_async_copy(ref, g.at[2 * src + column], sems.at[i]))
    for copy in copies:
        copy.start()
    for copy in copies:
        copy.wait()


def pick(g, masks, b):
    head = g[:, pl.ds(pl.multiple_of(b * 16, 16), 16), :]
    rest = g[:, pl.ds(pl.multiple_of(MAIN + (b // 4) * 16, 16), 16), :]
    rest = rest * masks[lax.rem(b, 4)][None]
    return jnp.concatenate(
        [head.reshape(SHARDS * 16, BLOCK), rest.reshape(SHARDS * 16, BLOCK)], 0)


def pick_two(g, masks, rows, c, s):
    return jnp.concatenate([pick(g, masks, rows[c, s]), pick(g, masks, rows[c, s + 1])], 1)


def weight_kernel(meta, rows, counts, masks, *refs):
    moved, refs = refs[:SHARDS], refs[SHARDS:]
    hid_t, keep, send, g, tiles, sems = refs
    load_shards(meta, moved, g, sems)
    core = meta[2]
    total = jnp.int32(0)
    for c in range(COLS):
        n = counts[c]

        def body(t, carry, c=c, first=total):
            s = 6 * t
            h = hid_t[c * BLOCK:(c + 1) * BLOCK, :]
            ws = [jnp.dot(h, pick_two(g, masks, rows, c, s + i), preferred_element_type=jnp.float32)
                  for i in (0, 2, 4)]
            for i, w in enumerate(ws):
                tiles[first + s + 2 * i] = w[:, :BLOCK].T
                tiles[first + s + 2 * i + 1] = w[:, BLOCK:].T
            return carry

        lax.fori_loop(0, (n + 5) // 6, body, 0)
        total = total + n

    sub = lax.broadcasted_iota(jnp.int32, (GROUPS, 8, BLOCK), 1)

    def pack(q, most):
        a = jnp.where(2 * q < total, tiles[2 * q].reshape(GROUPS, 8, BLOCK), 0.0)
        b = jnp.where(2 * q + 1 < total, tiles[2 * q + 1].reshape(GROUPS, 8, BLOCK), 0.0)
        lo = jnp.where(sub < 4, a, pltpu.roll(b, 4, 1))
        hi = jnp.where(sub < 4, pltpu.roll(a, 4, 1), b)
        keep[:, q] = jnp.where(core == 0, lo, hi)
        send[:, q] = jnp.where(core == 0, hi, lo)
        return jnp.maximum(most, jnp.max(jnp.maximum(jnp.abs(a), jnp.abs(b)), axis=0))

    most = lax.fori_loop(0, PAIRS, pack, jnp.zeros((8, BLOCK), jnp.float32))
    bound = jnp.full((4, BLOCK), jnp.max(most))
    for grp in range(GROUPS):
        keep[grp, PAIRS - 1, 4:8] = bound
        send[grp, PAIRS - 1, 4:8] = bound


def hidden_kernel(meta, rows, counts, masks, *refs):
    moved, refs = refs[:SHARDS], refs[SHARDS:]
    wts, gh_main, gh_tail, g, acc, sems = refs
    load_shards(meta, moved, g, sems)
    for c in range(COLS):
        n = counts[c]

        def part(s, c=c, n=n):
            parts = [wts[c, s]]
            for i in (1, 2, 3):
                w = wts[c, s + i]
                parts.append(jnp.where(s + i < n, w, jnp.zeros_like(w)))
            picked = jnp.concatenate(
                [pick_two(g, masks, rows, c, s), pick_two(g, masks, rows, c, s + 2)], 1)
            return jnp.dot(picked, jnp.concatenate(parts, 0), preferred_element_type=jnp.float32)

        acc[...] = part(0)

        def body(t, carry, part=part):
            acc[...] += part(4 * t)
            return carry

        lax.fori_loop(1, (n + 3) // 4, body, 0)
        cols = slice(c * BLOCK, (c + 1) * BLOCK)
        gh_main[:, :, cols] = acc[:SHARDS * 16].reshape(SHARDS, 16, BLOCK).astype(jnp.bfloat16)
        t = acc[SHARDS * 16:].reshape(SHARDS, 16, BLOCK)
        gh_tail[:, :, cols] = (t[:, 0:4] + t[:, 4:8]) + (t[:, 8:12] + t[:, 12:16])


def shards(grad_out, hidden, weight_tiles, row_list, counts):
    z, yl, core = lax.axis_index("z"), lax.axis_index("yl"), lax.axis_index("c")
    meta = jnp.stack([z, yl, core]).astype(jnp.int32)
    masks = np.repeat(np.eye(4), 4, axis=1)[:, :, None].repeat(BLOCK, axis=2)
    masks = jnp.asarray(masks.astype(ml_dtypes.bfloat16))

    shard = pack_rows(grad_out[0].reshape(TOK, DBLK, BLOCK))
    other = lax.ppermute(shard, "yl", ring(NYL, 1))
    moved = []
    for mine in (True, False):
        start = shard if mine else other
        up = down = start
        moved.append(start)
        for k in range(6):
            if k < 5 or mine:
                up = lax.ppermute(up, "z", ring(NZ, 1))
                moved.append(up)
            if k < 5 or not mine:
                down = lax.ppermute(down, "z", ring(NZ, -1))
                moved.append(down)
            if k == 0 and mine:
                other, down = lax.optimization_barrier((other, down))

    t = lax.broadcasted_iota(jnp.int32, (SHARDS * TOK, SHARDS * 32), 0)
    k = lax.broadcasted_iota(jnp.int32, (SHARDS * TOK, SHARDS * 32), 1)
    j = k % (SHARDS * 16)
    place = j // 16 * TOK + jnp.where(k < SHARDS * 16, j % 16, 16 + j % 4)
    hid_t = lax.dot_general(hidden[0], (t == place).astype(jnp.bfloat16), (((0,), (0,)), ((), ())))

    any_spec = pl.BlockSpec(memory_space=pl.ANY)
    smem = pl.BlockSpec(memory_space=pltpu.SMEM)
    vmem = pl.BlockSpec(memory_space=pltpu.VMEM)
    params = pltpu.CompilerParams(vmem_limit_bytes=62 * 1024 * 1024)
    shard_scratch = pltpu.VMEM((SHARDS, ROWS, BLOCK), jnp.bfloat16)
    keep, send = pl.pallas_call(
        weight_kernel,
        in_specs=[smem] * 3 + [vmem] + [any_spec] * SHARDS + [vmem],
        out_specs=[vmem] * 2,
        out_shape=[jax.ShapeDtypeStruct((GROUPS, PAIRS, 8, BLOCK), jnp.float32)] * 2,
        scratch_shapes=[
            shard_scratch,
            pltpu.VMEM((LIVE + 5, BLOCK, BLOCK), jnp.float32),
            pltpu.SemaphoreType.DMA((SHARDS,)),
        ],
        compiler_params=params,
        cost_estimate=pl.CostEstimate(flops=10**9, bytes_accessed=11 * 10**6, transcendentals=0),
        name="weight_grad",
    )(meta, row_list, counts, masks, *moved, hid_t)

    got = lax.ppermute(send, "c", ring(NC, 1))
    bound = keep[:, PAIRS - 1:, 4:5] + got[:, PAIRS - 1:, 4:5]
    power = jnp.clip(jnp.ceil(jnp.log2(bound)), -100.0, 30.0)
    at_pair = lax.broadcasted_iota(jnp.int32, keep.shape, 1)
    at_row = lax.broadcasted_iota(jnp.int32, keep.shape, 2)
    spare = (at_pair == PAIRS - 1) & (at_row >= 4)
    coded = jnp.where(spare, power, (keep + got) * jnp.exp2(14.0 - power)).astype(jnp.float16)
    coded, meta_after = lax.optimization_barrier((coded, meta))
    parts = lax.all_to_all(coded, ("yh", "x"), 0, 0, tiled=True)

    gh_main, gh_tail = pl.pallas_call(
        hidden_kernel,
        in_specs=[smem] * 3 + [vmem] + [any_spec] * SHARDS + [vmem],
        out_specs=[vmem] * 2,
        out_shape=[
            jax.ShapeDtypeStruct((SHARDS, 16, COLS * BLOCK), jnp.bfloat16),
            jax.ShapeDtypeStruct((SHARDS, 4, COLS * BLOCK), jnp.float32),
        ],
        scratch_shapes=[
            shard_scratch,
            pltpu.VMEM((SHARDS * 32, BLOCK), jnp.float32),
            pltpu.SemaphoreType.DMA((SHARDS,)),
        ],
        compiler_params=params,
        cost_estimate=pl.CostEstimate(flops=10**9, bytes_accessed=10 * 10**6, transcendentals=0),
        name="hidden_grad",
    )(meta_after, row_list, counts, masks, *moved, weight_tiles)

    undo = jnp.exp2(parts[:, PAIRS - 1:, 4:5].astype(jnp.float32) - 14.0) * NORM
    packed = jnp.sum(parts.astype(jnp.float32) * undo, axis=0)
    packed = jnp.where(spare[0], 0.0, packed).reshape(2 * PAIRS, 4, BLOCK)

    slot = lax.broadcasted_iota(jnp.int32, (COLS, SLOTS), 1)
    live = slot < counts[:, None]
    first = jnp.cumsum(counts) - counts
    place = jnp.where(live, first[:, None] + slot, 2 * PAIRS - 1)
    grad_tiles = jnp.take(packed, place.reshape(-1), axis=0, mode="clip")
    grad_tiles = grad_tiles.reshape(COLS, SLOTS, 4, BLOCK)

    grad_hidden = jnp.concatenate([gh_main, gh_tail.astype(jnp.bfloat16)], axis=1)
    return grad_hidden.reshape(1, SHARDS * TOK, COLS * BLOCK), grad_tiles


def solution(mesh):
    fine = Mesh(mesh.devices.reshape(NZ, NYL, NYH, NX, NC), ("z", "yl", "yh", "x", "c"))
    tp, dp = ("z", "yl"), ("yh", "x", "c")
    return jax.shard_map(
        shards,
        mesh=fine,
        in_specs=(
            P(dp, tp, None),
            P(dp, None, tp),
            P(tp, None, None, None),
            P(tp, None),
            P(tp),
        ),
        out_specs=(P(dp, None, tp), P(tp, None, dp, None)),
        check_vma=False,
    )
```
